32 devices in a mesh: pool: 2 (over x), row: 8 (over z, y), col: 2 (over core).
Axes of the slice: x: 2, y: 2, z: 4, core: 2. Of those that a mesh axis runs over, the one named last changes fastest.
Arguments:
- row_features: bfloat16 [128, 32768], P('col', ('pool', 'row')), parts along dimension 1, may hold values from -6 to 6
- col_features: bfloat16 [128, 16384], P('row', ('pool', 'col')), parts along dimension 1, may hold values from -6 to 6
- solve_rows: float32 [32768], P(('pool', 'row')), parts along dimension 0, may hold values from -16 to 16
- solve_cols: float32 [16384], P(('pool', 'col')), parts along dimension 0, may hold values from -16 to 16
- probe_rows: float32 [16, 32768], P(None, ('pool', 'row')), parts along dimension 1, may hold values from -16 to 16
- probe_cols: float32 [16, 16384], P(None, ('pool', 'col')), parts along dimension 1, may hold values from -12 to 12
Outputs:
- row_grad: float32 [128, 32768], P('col', ('pool', 'row')), parts along dimension 1
- col_grad: float32 [128, 16384], P('row', ('pool', 'col')), parts along dimension 1
The draws below stay inside these ranges and needn't reach their ends.
There are 2 independent parts, one for each index of `pool`. The reference program is written for one: setup_inputs(seed, part) draws one part's arguments, and reference() takes and returns one part's arrays. A program takes and returns all parts, laid end to end along the dimension named above; each array names one. Nothing has to cross between parts.
All inputs are finite; a program needn't handle non-finite values.
Results may differ from the reference program's by a relative error of at most 0.0022.
Values may be sent and summed in bfloat16 or wider, within the bound.
A program may use at most 64 MiB of HBM per device.

```python
import jax
import jax.numpy as jnp
from jax import lax

FEATURES = 128
PROBES = 16
ROWS = 16384
COLS = 8192


def block_levels(key, dims, cuts, low, high):
    loudness, own = 1.0, jax.random.fold_in(key, 6)
    for position, shards_of in cuts:
        draws = jnp.exp(jax.random.uniform(jax.random.fold_in(own, position), (shards_of,), jnp.float32, low / len(cuts), high / len(cuts)))
        loudness = loudness * jnp.repeat(draws, dims[position] // shards_of).reshape([-1 if axis == position else 1 for axis in range(len(dims))])
    return loudness


def noise(own_key, shape, spread, reach, split=(), dtype=jnp.bfloat16):
    array = spread * jax.random.normal(own_key, shape, jnp.float32)
    if split:
        array = array * block_levels(own_key, shape, split, -0.22, 0.18)
    return jnp.clip(array, -reach, reach).astype(dtype)


def setup_inputs(seed: int = 0, part: int = 0) -> dict:
    splits = jax.random.split(jax.random.key(seed), 7)
    own_keys = jax.random.split(jax.random.fold_in(splits[6], part), 7)
    return {
        "row_features": noise(own_keys[0], (FEATURES, ROWS), 1.0, 6.0, ((0, 2), (1, 8))),
        "col_features": noise(own_keys[1], (FEATURES, COLS), 1.0, 6.0, ((0, 8), (1, 2))),
        "solve_rows": noise(own_keys[2], (ROWS,), 3.0, 16.0, ((0, 8),), jnp.float32),
        "solve_cols": noise(own_keys[3], (COLS,), 3.0, 16.0, ((0, 2),), jnp.float32),
        "probe_rows": noise(own_keys[4], (PROBES, ROWS), 4.0, 16.0, ((1, 8),), jnp.float32),
        "probe_cols": noise(own_keys[5], (PROBES, COLS), 2.0, 12.0, ((1, 2),), jnp.float32),
    }


def reference(row_features, col_features, solve_rows, solve_cols, probe_rows, probe_cols):
    highest = lax.Precision.HIGHEST
    inverse_sq = 4.0 / FEATURES
    row_weight = jnp.concatenate([0.5 * solve_rows[None, :], (-0.5 / PROBES) * probe_rows], 0).astype(jnp.float32)
    col_weight = jnp.concatenate([solve_cols[None, :], probe_cols], 0).astype(jnp.float32)
    rows_wide = row_features.astype(jnp.float32)
    row_norm = jnp.sum(rows_wide * rows_wide, 0)
    block_size = min(COLS, 1024)
    turn_count = COLS // block_size
    col_blocks = col_features.reshape(FEATURES, turn_count, block_size).transpose(1, 0, 2)
    weight_blocks = col_weight.reshape(PROBES + 1, turn_count, block_size).transpose(1, 0, 2)

    def one_turn(state_now, pieces):
        row_acc, row_sum = state_now
        q_features, q_weight = pieces
        q_wide = q_features.astype(jnp.float32)
        cross_term = jnp.dot(rows_wide.T, q_wide, precision=highest)
        sq_dist = row_norm[:, None] + jnp.sum(q_wide * q_wide, 0)[None, :] - 2.0 * cross_term
        kernel_tile = jnp.exp(-0.5 * inverse_sq * sq_dist)
        coupling = jnp.dot(row_weight.T, q_weight, precision=highest)
        weighted = coupling * kernel_tile
        weighted_bf = lax.optimization_barrier(weighted.astype(jnp.bfloat16)).astype(jnp.float32)
        row_acc = row_acc + jnp.dot(q_wide, weighted_bf.T, precision=highest)
        row_sum = row_sum + jnp.sum(weighted, 1)
        col_part = inverse_sq * (jnp.dot(rows_wide, weighted_bf, precision=highest) - q_wide * jnp.sum(weighted, 0)[None, :])
        return (row_acc, row_sum), col_part

    initial = (jnp.zeros((FEATURES, ROWS), jnp.float32), jnp.zeros((ROWS,), jnp.float32))
    (row_acc, row_sum), col_parts = lax.scan(one_turn, initial, (col_blocks, weight_blocks))
    row_grad = inverse_sq * (row_acc - rows_wide * row_sum[None, :])
    col_grad = col_parts.transpose(1, 0, 2).reshape(FEATURES, COLS)
    return row_grad, col_grad
```

```python
import functools

import jax
import jax.numpy as jnp
from jax import lax
from jax.experimental import pallas as pl
from jax.experimental.pallas import tpu as pltpu
from jax.sharding import PartitionSpec as P

FEATURES = 128
PROBES = 16
WIDE = FEATURES + 16
WEIGHT_ROWS = 64
STRIP = 512
ROW_TILE = 256
COL_TILE = 512
LOG2E = 1.4426950408889634
F32 = jnp.float32
BF16 = jnp.bfloat16


def split_parts(values, count):
    parts = []
    for _ in range(count - 1):
        high = values.astype(BF16).astype(F32)
        parts.append(high)
        values = values - high
    parts.append(values)
    return parts


def half_norm(features):
    wide = features.astype(F32)
    return jnp.concatenate(split_parts(-0.5 * jnp.sum(wide * wide, 0, keepdims=True), 3), 0)


def extra_rows(features, norm_first):
    count = features.shape[1]
    ones = jnp.ones((3, count), F32)
    pad = jnp.zeros((WIDE - FEATURES - 6, count), F32)
    norm = half_norm(features)
    rows = [norm, ones, pad] if norm_first else [ones, norm, pad]
    return jnp.concatenate(rows, 0).astype(BF16)


def weight_rows(solve, probe, solve_scale, probe_scale, low_last):
    high, low = split_parts(jnp.concatenate([solve_scale * solve, probe_scale * probe], 0), 2)
    pad = jnp.zeros((WEIGHT_ROWS - 3 * (PROBES + 1), solve.shape[1]), F32)
    parts = [high, high, low] if low_last else [high, low, high]
    return jnp.concatenate(parts + [pad], 0).astype(BF16)


def window(index_now, size):
    return pl.ds(pl.multiple_of(index_now * size, size), size)


def turned(values):
    return values.astype(F32).T.astype(BF16)


def local_kernel(
    x_ref, z_ref, sr_ref, sc_ref, pr_ref, pc_ref, row_ref, col_ref,
    x_aug, z_aug, x_turn, rw_turn, c_weight, row_acc, col_acc,
):
    inverse_sq = 4.0 / FEATURES
    row_count, col_count = x_ref.shape[1], z_ref.shape[1]
    row_tiles = row_count // ROW_TILE

    @pl.loop(0, row_count // STRIP)
    def _(index_now):
        at = window(index_now, STRIP)
        x = x_ref[:, at]
        x_aug[0:FEATURES, at] = x
        x_aug[FEATURES:WIDE, at] = extra_rows(x, False)
        x_turn[at, :] = turned(x_aug[:, at])
        rw_turn[at, :] = turned(weight_rows(sr_ref[:, at], pr_ref[:, at], 0.5, -0.5 / PROBES, False))

    @pl.loop(0, col_count // STRIP)
    def _(index_now):
        at = window(index_now, STRIP)
        z = z_ref[:, at]
        z_aug[0:FEATURES, at] = z
        z_aug[FEATURES:WIDE, at] = extra_rows(z, True)
        c_weight[:, at] = weight_rows(sc_ref[:, at], pc_ref[:, at], 1.0, 1.0, True)

    row_acc[...] = jnp.zeros_like(row_acc)

    def weighted_tile(i, at_j):
        at_i = pl.ds(i * ROW_TILE, ROW_TILE)
        half = jnp.dot(x_turn[at_i, :], z_aug[:, at_j], preferred_element_type=F32)
        coupling = jnp.dot(rw_turn[at_i, :], c_weight[:, at_j], preferred_element_type=F32)
        return (coupling * jnp.exp2(half * (inverse_sq * LOG2E))).astype(BF16)

    @pl.loop(0, col_count // COL_TILE)
    def _(j):
        at_j = window(j, COL_TILE)
        weighted = weighted_tile(0, at_j)
        for i in range(row_tiles):
            following = weighted_tile(i + 1, at_j) if i + 1 < row_tiles else None
            at_i = pl.ds(i * ROW_TILE, ROW_TILE)
            row_acc[:, at_i] += lax.dot_general(
                z_aug[:, at_j], weighted, (((1,), (1,)), ((), ())), preferred_element_type=F32
            )
            part = jnp.dot(x_aug[:, at_i], weighted, preferred_element_type=F32)
            if i == 0:
                col_acc[...] = part
            else:
                col_acc[...] += part
            weighted = following
        col_ref[:, at_j] = inverse_sq * (
            col_acc[0:FEATURES, :] - z_ref[:, at_j].astype(F32) * col_acc[FEATURES:FEATURES + 1, :]
        )

    @pl.loop(0, row_count // STRIP)
    def _(index_now):
        at = window(index_now, STRIP)
        row_ref[:, at] = inverse_sq * (
            row_acc[0:FEATURES, at] - x_ref[:, at].astype(F32) * row_acc[FEATURES + 3:FEATURES + 4, at]
        )


def shards(row_features, col_features, solve_rows, solve_cols, probe_rows, probe_cols):
    row_count, col_count = row_features.shape[1], col_features.shape[1]
    row_full = lax.all_gather(row_features, "col", axis=0, tiled=True)
    col_full = lax.all_gather(col_features, "row", axis=0, tiled=True)
    vmem = pl.BlockSpec(memory_space=pltpu.VMEM)
    row_part, col_part = pl.pallas_call(
        local_kernel,
        out_shape=(
            jax.ShapeDtypeStruct((FEATURES, row_count), F32),
            jax.ShapeDtypeStruct((FEATURES, col_count), F32),
        ),
        in_specs=[vmem] * 6,
        out_specs=(vmem, vmem),
        scratch_shapes=[
            pltpu.VMEM((WIDE, row_count), BF16),
            pltpu.VMEM((WIDE, col_count), BF16),
            pltpu.VMEM((row_count, WIDE), BF16),
            pltpu.VMEM((row_count, WEIGHT_ROWS), BF16),
            pltpu.VMEM((WEIGHT_ROWS, col_count), BF16),
            pltpu.VMEM((WIDE, row_count), F32),
            pltpu.VMEM((WIDE, COL_TILE), F32),
        ],
        compiler_params=pltpu.CompilerParams(vmem_limit_bytes=48 * 2**20),
        name="local_sweep",
    )(row_full, col_full, solve_rows[None, :], solve_cols[None, :], probe_rows, probe_cols)
    col_grad = lax.psum_scatter(col_part, "row", scatter_dimension=0, tiled=True)
    row_grad = lax.psum_scatter(row_part, "col", scatter_dimension=0, tiled=True)
    return (row_grad, col_grad)


def solution(mesh):
    return jax.shard_map(
        shards,
        mesh=mesh,
        in_specs=(
            P("col", ("pool", "row")),
            P("row", ("pool", "col")),
            P(("pool", "row")),
            P(("pool", "col")),
            P(None, ("pool", "row")),
            P(None, ("pool", "col")),
        ),
        out_specs=(P("col", ("pool", "row")), P("row", ("pool", "col"))),
        check_vma=False,
    )
```

```python
import functools

import jax
import jax.numpy as jnp
from jax import lax
from jax.experimental import pallas as pl
from jax.experimental.pallas import tpu as pltpu
from jax.sharding import PartitionSpec as P

FEATURES = 128
PROBES = 16
WIDE = FEATURES + 16
WEIGHT_ROWS = 64
STRIP = 512
ROW_TILE = 256
COL_TILE = 512
AHEAD = 2
LOG2E = 1.4426950408889634
F32 = jnp.float32
BF16 = jnp.bfloat16


def split_parts(values, count):
    parts = []
    for _ in range(count - 1):
        high = values.astype(BF16).astype(F32)
        parts.append(high)
        values = values - high
    parts.append(values)
    return parts


def half_norm(features):
    wide = features.astype(F32)
    return jnp.concatenate(split_parts(-0.5 * jnp.sum(wide * wide, 0, keepdims=True), 3), 0)


def extra_rows(features, norm_first):
    count = features.shape[1]
    ones = jnp.ones((3, count), F32)
    pad = jnp.zeros((WIDE - FEATURES - 6, count), F32)
    norm = half_norm(features)
    rows = [norm, ones, pad] if norm_first else [ones, norm, pad]
    return jnp.concatenate(rows, 0).astype(BF16)


def weight_rows(solve, probe, solve_scale, probe_scale, low_last):
    high, low = split_parts(jnp.concatenate([solve_scale * solve, probe_scale * probe], 0), 2)
    pad = jnp.zeros((WEIGHT_ROWS - 3 * (PROBES + 1), solve.shape[1]), F32)
    parts = [high, high, low] if low_last else [high, low, high]
    return jnp.concatenate(parts + [pad], 0).astype(BF16)


def window(index_now, size):
    return pl.ds(pl.multiple_of(index_now * size, size), size)


def turned(values):
    return values.astype(F32).T.astype(BF16)


def local_kernel(
    x_ref, z_ref, sr_ref, sc_ref, pr_ref, pc_ref, row_ref, col_ref,
    x_aug, z_aug, x_turn, rw_turn, c_weight, row_acc, col_acc,
):
    inverse_sq = 4.0 / FEATURES
    row_count, col_count = x_ref.shape[1], z_ref.shape[1]
    row_tiles = row_count // ROW_TILE

    @pl.loop(0, row_count // STRIP)
    def _(index_now):
        at = window(index_now, STRIP)
        x = x_ref[:, at]
        x_aug[0:FEATURES, at] = x
        x_aug[FEATURES:WIDE, at] = extra_rows(x, False)
        x_turn[at, :] = turned(x_aug[:, at])
        rw_turn[at, :] = turned(weight_rows(sr_ref[:, at], pr_ref[:, at], 0.5, -0.5 / PROBES, False))

    @pl.loop(0, col_count // STRIP)
    def _(index_now):
        at = window(index_now, STRIP)
        z = z_ref[:, at]
        z_aug[0:FEATURES, at] = z
        z_aug[FEATURES:WIDE, at] = extra_rows(z, True)
        c_weight[:, at] = weight_rows(sc_ref[:, at], pc_ref[:, at], 1.0, 1.0, True)

    row_acc[...] = jnp.zeros_like(row_acc)

    def weighted_tile(i, at_j):
        at_i = pl.ds(i * ROW_TILE, ROW_TILE)
        half = jnp.dot(x_turn[at_i, :], z_aug[:, at_j], preferred_element_type=F32)
        coupling = jnp.dot(rw_turn[at_i, :], c_weight[:, at_j], preferred_element_type=F32)
        return (coupling * jnp.exp2(half * (inverse_sq * LOG2E))).astype(BF16)

    @pl.loop(0, col_count // COL_TILE)
    def _(j):
        at_j = window(j, COL_TILE)
        weighted = weighted_tile(0, at_j)
        for i in range(row_tiles):
            following = weighted_tile(i + 1, at_j) if i + 1 < row_tiles else None
            at_i = pl.ds(i * ROW_TILE, ROW_TILE)
            row_acc[:, at_i] += lax.dot_general(
                z_aug[:, at_j], weighted, (((1,), (1,)), ((), ())), preferred_element_type=F32
            )
            part = jnp.dot(x_aug[:, at_i], weighted, preferred_element_type=F32)
            if i == 0:
                col_acc[...] = part
            else:
                col_acc[...] += part
            weighted = following
        col_ref[:, at_j] = inverse_sq * (
            col_acc[0:FEATURES, :] - z_ref[:, at_j].astype(F32) * col_acc[FEATURES:FEATURES + 1, :]
        )

    @pl.loop(0, row_count // STRIP)
    def _(index_now):
        at = window(index_now, STRIP)
        row_ref[:, at] = inverse_sq * (
            row_acc[0:FEATURES, at] - x_ref[:, at].astype(F32) * row_acc[FEATURES + 3:FEATURES + 4, at]
        )


def shards(row_features, col_features, solve_rows, solve_cols, probe_rows, probe_cols):
    row_count, col_count = row_features.shape[1], col_features.shape[1]
    row_full = lax.all_gather(row_features, "col", axis=0, tiled=True)
    col_full = lax.all_gather(col_features, "row", axis=0, tiled=True)
    vmem = pl.BlockSpec(memory_space=pltpu.VMEM)
    row_part, col_part = pl.pallas_call(
        local_kernel,
        out_shape=(
            jax.ShapeDtypeStruct((FEATURES, row_count), F32),
            jax.ShapeDtypeStruct((FEATURES, col_count), F32),
        ),
        in_specs=[vmem] * 6,
        out_specs=(vmem, vmem),
        scratch_shapes=[
            pltpu.VMEM((WIDE, row_count), BF16),
            pltpu.VMEM((WIDE, col_count), BF16),
            pltpu.VMEM((row_count, WIDE), BF16),
            pltpu.VMEM((row_count, WEIGHT_ROWS), BF16),
            pltpu.VMEM((WEIGHT_ROWS, col_count), BF16),
            pltpu.VMEM((WIDE, row_count), F32),
            pltpu.VMEM((WIDE, COL_TILE), F32),
        ],
        compiler_params=pltpu.CompilerParams(vmem_limit_bytes=48 * 2**20),
        name="local_sweep",
    )(row_full, col_full, solve_rows[None, :], solve_cols[None, :], probe_rows, probe_cols)
    col_grad = lax.psum_scatter(col_part, "row", scatter_dimension=0, tiled=True)
    row_grad = lax.psum_scatter(row_part, "col", scatter_dimension=0, tiled=True)
    return (row_grad, col_grad)


def fused_kernel(
    pair_count, x_ref, z_ref, sr_ref, sc_ref, pr_ref, pc_ref, row_ref, col_ref,
    x_aug, z_aug, x_turn, rw_turn, c_weight, row_acc, col_acc,
    col_part, pair_send, pair_recv, line_send, line_recv, row_send, row_recv,
    x_sems, own_send_sems, pass_send_sems, line_in, pair_in,
    pair_send_sem, pair_sum_in, line_send_sems, line_sum_in, row_send_sem, row_in,
):
    inverse_sq = 4.0 / FEATURES
    row_count, col_count = x_ref.shape[1], z_ref.shape[1]
    x_rows, z_rows = x_ref.shape[0], z_ref.shape[0]
    row_tiles, chunks = row_count // ROW_TILE, col_count // COL_TILE
    others = pair_count - 1
    me_row, me_col = lax.axis_index("row"), lax.axis_index("col")
    side, place = lax.rem(me_row, 2), me_row // 2
    pair_row = 2 * place + 1 - side
    other_col = 1 - me_col

    def line_place(step):
        return lax.rem(place + step, pair_count)

    def piece(owner, size):
        return pl.ds(pl.multiple_of(owner * size, size), size)

    def send(src, dst, send_sem, recv_sem, where):
        return pltpu.make_async_remote_copy(
            src_ref=src, dst_ref=dst, send_sem=send_sem, recv_sem=recv_sem,
            device_id=where, device_id_type=pl.DeviceIdType.MESH,
        )

    barrier = pltpu.get_barrier_semaphore()
    partners = [{"col": other_col}, {"row": pair_row}]
    partners += [{"row": 2 * line_place(k) + side} for k in range(1, pair_count)]
    for partner in partners:
        pl.semaphore_signal(barrier, inc=1, device_id=partner, device_id_type=pl.DeviceIdType.MESH)
    pl.semaphore_wait(barrier, len(partners))

    my_x = piece(me_col, x_rows)
    x_copy = send(x_ref, x_aug.at[my_x, :], x_sems.at[0], x_sems.at[1], {"col": other_col})
    my_z = piece(me_row, z_rows)

    def own_copy(k, at, recv_sem):
        where = pair_row if k == 0 else 2 * line_place(k) + side
        return send(z_ref.at[:, at], z_aug.at[my_z, at], own_send_sems.at[k], recv_sem, {"row": where})

    def pass_copy(k, at, recv_sem):
        owner = piece(2 * line_place(k) + side, z_rows)
        return send(z_aug.at[owner, at], z_aug.at[owner, at], pass_send_sems.at[k - 1], recv_sem, {"row": pair_row})

    @pl.loop(0, chunks)
    def _(c):
        at = window(c, COL_TILE)
        for k in range(1, pair_count):
            own_copy(k, at, line_in.at[c]).start()
        own_copy(0, at, pair_in.at[c]).start()
        @pl.when(c == 0)
        def _():
            x_copy.start()

    def take_line(c):
        at = window(c, COL_TILE)
        got = z_aug.at[pl.ds(0, others * z_rows), at]
        pltpu.make_async_copy(got, got, line_in.at[c]).wait()
        for k in range(1, pair_count):
            pass_copy(k, at, pair_in.at[c]).start()

    def take_pair(c):
        got = z_aug.at[pl.ds(0, pair_count * z_rows), window(c, COL_TILE)]
        pltpu.make_async_copy(got, got, pair_in.at[c]).wait()

    z_aug[my_z, :] = z_ref[...]
    x_aug[my_x, :] = x_ref[...]

    @pl.loop(0, row_count // STRIP)
    def _(index_now):
        at = window(index_now, STRIP)
        rw_turn[at, :] = turned(weight_rows(sr_ref[:, at], pr_ref[:, at], 0.5, -0.5 / PROBES, False))

    row_acc[...] = jnp.zeros_like(row_acc)
    x_copy.wait_recv()

    @pl.loop(0, row_count // STRIP)
    def _(index_now):
        at = window(index_now, STRIP)
        x_aug[FEATURES:WIDE, at] = extra_rows(x_aug[0:FEATURES, at], False)
        x_turn[at, :] = turned(x_aug[:, at])

    for c in range(min(AHEAD, chunks)):
        take_line(c)

    def weighted_tile(i, at_j):
        at_i = pl.ds(i * ROW_TILE, ROW_TILE)
        half = jnp.dot(x_turn[at_i, :], z_aug[:, at_j], preferred_element_type=F32)
        coupling = jnp.dot(rw_turn[at_i, :], c_weight[...], preferred_element_type=F32)
        return (coupling * jnp.exp2(half * (inverse_sq * LOG2E))).astype(BF16)

    def pair_copy(c):
        return send(pair_send.at[c], pair_recv.at[c], pair_send_sem, pair_sum_in.at[c], {"row": pair_row})

    def line_copy(c, k):
        return send(
            line_send.at[c, k - 1], line_recv.at[c, k - 1], line_send_sems.at[k - 1], line_sum_in.at[c],
            {"row": 2 * line_place(k) + side},
        )

    def add_pair(c):
        pltpu.make_async_copy(pair_recv.at[c], pair_recv.at[c], pair_sum_in.at[c]).wait()
        for k in range(1, pair_count):
            there = line_place(k)
            total = col_part[c, piece(2 * there + side, z_rows), :] + pair_recv[c, there]
            line_send[c, k - 1] = total
            line_copy(c, k).start()

    def add_line(c):
        pltpu.make_async_copy(line_recv.at[c], line_recv.at[c], line_sum_in.at[c]).wait()
        total = col_part[c, my_z, :] + pair_recv[c, place]
        for k in range(1, pair_count):
            total = total + line_recv[c, k - 1]
        col_ref[:, window(c, COL_TILE)] = total

    @pl.loop(0, chunks)
    def _(c):
        at_j = window(c, COL_TILE)

        @pl.when(c + AHEAD < chunks)
        def _():
            take_line(c + AHEAD)

        c_weight[...] = weight_rows(sc_ref[:, at_j], pc_ref[:, at_j], 1.0, 1.0, True)
        take_pair(c)
        z_aug[FEATURES:WIDE, at_j] = extra_rows(z_aug[0:FEATURES, at_j], True)
        weighted = weighted_tile(0, at_j)
        for i in range(row_tiles):
            following = weighted_tile(i + 1, at_j) if i + 1 < row_tiles else None
            at_i = pl.ds(i * ROW_TILE, ROW_TILE)
            row_acc[:, at_i] += lax.dot_general(
                z_aug[:, at_j], weighted, (((1,), (1,)), ((), ())), preferred_element_type=F32
            )
            part = jnp.dot(x_aug[:, at_i], weighted, preferred_element_type=F32)
            if i == 0:
                col_acc[...] = part
            else:
                col_acc[...] += part
            weighted = following
        col_part[c] = inverse_sq * (
            col_acc[0:FEATURES, :] - z_aug[0:FEATURES, at_j].astype(F32) * col_acc[FEATURES:FEATURES + 1, :]
        )
        for there in range(pair_count):
            pair_send[c, there] = col_part[c, piece(2 * there + 1 - side, z_rows), :]
        pair_copy(c).start()

        @pl.when(c >= 1)
        def _():
            add_pair(c - 1)

    def row_piece(owner, at):
        at_f = piece(owner, x_rows)
        return inverse_sq * (
            row_acc[at_f, at] - x_aug[at_f, at].astype(F32) * row_acc[FEATURES + 3:FEATURES + 4, at]
        )

    def row_copy(index_now):
        return send(
            row_send.at[index_now], row_recv.at[index_now], row_send_sem, row_in.at[index_now], {"col": other_col}
        )

    strips = row_count // STRIP

    @pl.loop(0, strips)
    def _(index_now):
        row_send[index_now] = row_piece(other_col, window(index_now, STRIP))
        row_copy(index_now).start()

    add_pair(chunks - 1)

    @pl.loop(0, chunks - 1)
    def _(c):
        add_line(c)

    @pl.loop(0, strips)
    def _(index_now):
        at = window(index_now, STRIP)
        row_copy(index_now).wait_recv()
        row_ref[:, at] = row_piece(me_col, at) + row_recv[index_now]

    add_line(chunks - 1)

    x_copy.wait_send()
    for k in range(pair_count):
        own_copy(k, pl.ds(0, col_count), line_in.at[0]).wait_send()
    for k in range(1, pair_count):
        pass_copy(k, pl.ds(0, col_count), pair_in.at[0]).wait_send()
        sent = line_send.at[:, k - 1]
        pltpu.make_async_copy(sent, sent, line_send_sems.at[k - 1]).wait()
    pltpu.make_async_copy(pair_send, pair_send, pair_send_sem).wait()
    pltpu.make_async_copy(row_send, row_send, row_send_sem).wait()


def fused_shards(rows, row_features, col_features, solve_rows, solve_cols, probe_rows, probe_cols):
    (x_rows, row_count), (z_rows, col_count) = row_features.shape, col_features.shape
    pair_count, chunks, strips = rows // 2, col_count // COL_TILE, row_count // STRIP
    vmem = pl.BlockSpec(memory_space=pltpu.VMEM)
    dma = pltpu.SemaphoreType.DMA
    return pl.pallas_call(
        functools.partial(fused_kernel, pair_count),
        out_shape=(
            jax.ShapeDtypeStruct((x_rows, row_count), F32),
            jax.ShapeDtypeStruct((z_rows, col_count), F32),
        ),
        in_specs=[vmem] * 6,
        out_specs=(vmem, vmem),
        scratch_shapes=[
            pltpu.VMEM((WIDE, row_count), BF16),
            pltpu.VMEM((WIDE, col_count), BF16),
            pltpu.VMEM((row_count, WIDE), BF16),
            pltpu.VMEM((row_count, WEIGHT_ROWS), BF16),
            pltpu.VMEM((WEIGHT_ROWS, COL_TILE), BF16),
            pltpu.VMEM((WIDE, row_count), F32),
            pltpu.VMEM((WIDE, COL_TILE), F32),
            pltpu.VMEM((chunks, FEATURES, COL_TILE), F32),
            pltpu.VMEM((chunks, pair_count, z_rows, COL_TILE), F32),
            pltpu.VMEM((chunks, pair_count, z_rows, COL_TILE), F32),
            pltpu.VMEM((chunks, pair_count - 1, z_rows, COL_TILE), F32),
            pltpu.VMEM((chunks, pair_count - 1, z_rows, COL_TILE), F32),
            pltpu.VMEM((strips, x_rows, STRIP), F32),
            pltpu.VMEM((strips, x_rows, STRIP), F32),
            dma((2,)),
            dma((pair_count,)),
            dma((pair_count - 1,)),
            dma((chunks,)),
            dma((chunks,)),
            dma,
            dma((chunks,)),
            dma((pair_count - 1,)),
            dma((chunks,)),
            dma,
            dma((strips,)),
        ],
        compiler_params=pltpu.CompilerParams(
            collective_id=0, has_side_effects=True, vmem_limit_bytes=48 * 2**20
        ),
        name="fused_sweep",
    )(row_features, col_features, solve_rows[None, :], solve_cols[None, :], probe_rows, probe_cols)


def solution(mesh):
    rows = mesh.shape["row"]
    whole_tiles = (FEATURES // rows) % 16 == 0 and rows >= 4 and rows % 2 == 0 and mesh.shape["col"] == 2
    return jax.shard_map(
        functools.partial(fused_shards, rows) if whole_tiles else shards,
        mesh=mesh,
        in_specs=(
            P("col", ("pool", "row")),
            P("row", ("pool", "col")),
            P(("pool", "row")),
            P(("pool", "col")),
            P(None, ("pool", "row")),
            P(None, ("pool", "col")),
        ),
        out_specs=(P("col", ("pool", "row")), P("row", ("pool", "col"))),
        check_vma=False,
    )
```

```python
import functools

import jax
import jax.numpy as jnp
from jax import lax
from jax.experimental import pallas as pl
from jax.experimental.pallas import tpu as pltpu
from jax.sharding import PartitionSpec as P

FEATURES = 128
PROBES = 16
WIDE = FEATURES + 16
WEIGHT_ROWS = 64
STRIP = 512
ROW_TILE = 256
COL_TILE = 1024
AHEAD = 2
SCALE_LANES = 128
LOG2E = 1.4426950408889634
F32 = jnp.float32
BF16 = jnp.bfloat16


def split_parts(values, count):
    parts = []
    for _ in range(count - 1):
        high = values.astype(BF16).astype(F32)
        parts.append(high)
        values = values - high
    parts.append(values)
    return parts


def half_norm(features):
    wide = features.astype(F32)
    return jnp.concatenate(split_parts(-0.5 * jnp.sum(wide * wide, 0, keepdims=True), 3), 0)


def extra_rows(features, norm_first):
    count = features.shape[1]
    ones = jnp.ones((3, count), F32)
    pad = jnp.zeros((WIDE - FEATURES - 6, count), F32)
    norm = half_norm(features)
    rows = [norm, ones, pad] if norm_first else [ones, norm, pad]
    return jnp.concatenate(rows, 0).astype(BF16)


def weight_rows(solve, probe, solve_scale, probe_scale, low_last):
    high, low = split_parts(jnp.concatenate([solve_scale * solve, probe_scale * probe], 0), 2)
    pad = jnp.zeros((WEIGHT_ROWS - 3 * (PROBES + 1), solve.shape[1]), F32)
    parts = [high, high, low] if low_last else [high, low, high]
    return jnp.concatenate(parts + [pad], 0).astype(BF16)


def window(index_now, size):
    return pl.ds(pl.multiple_of(index_now * size, size), size)


def turned(values):
    return values.astype(F32).T.astype(BF16)


def local_kernel(
    x_ref, z_ref, sr_ref, sc_ref, pr_ref, pc_ref, row_ref, col_ref,
    x_aug, z_aug, x_turn, rw_turn, c_weight, row_acc, col_acc,
):
    inverse_sq = 4.0 / FEATURES
    row_count, col_count = x_ref.shape[1], z_ref.shape[1]
    row_tiles = row_count // ROW_TILE

    @pl.loop(0, row_count // STRIP)
    def _(index_now):
        at = window(index_now, STRIP)
        x = x_ref[:, at]
        x_aug[0:FEATURES, at] = x
        x_aug[FEATURES:WIDE, at] = extra_rows(x, False)
        x_turn[at, :] = turned(x_aug[:, at])
        rw_turn[at, :] = turned(weight_rows(sr_ref[:, at], pr_ref[:, at], 0.5, -0.5 / PROBES, False))

    @pl.loop(0, col_count // STRIP)
    def _(index_now):
        at = window(index_now, STRIP)
        z = z_ref[:, at]
        z_aug[0:FEATURES, at] = z
        z_aug[FEATURES:WIDE, at] = extra_rows(z, True)
        c_weight[:, at] = weight_rows(sc_ref[:, at], pc_ref[:, at], 1.0, 1.0, True)

    row_acc[...] = jnp.zeros_like(row_acc)

    def weighted_tile(i, at_j):
        at_i = pl.ds(i * ROW_TILE, ROW_TILE)
        half = jnp.dot(x_turn[at_i, :], z_aug[:, at_j], preferred_element_type=F32)
        coupling = jnp.dot(rw_turn[at_i, :], c_weight[:, at_j], preferred_element_type=F32)
        return (coupling * jnp.exp2(half * (inverse_sq * LOG2E))).astype(BF16)

    @pl.loop(0, col_count // COL_TILE)
    def _(j):
        at_j = window(j, COL_TILE)
        weighted = weighted_tile(0, at_j)
        for i in range(row_tiles):
            following = weighted_tile(i + 1, at_j) if i + 1 < row_tiles else None
            at_i = pl.ds(i * ROW_TILE, ROW_TILE)
            row_acc[:, at_i] += lax.dot_general(
                z_aug[:, at_j], weighted, (((1,), (1,)), ((), ())), preferred_element_type=F32
            )
            part = jnp.dot(x_aug[:, at_i], weighted, preferred_element_type=F32)
            if i == 0:
                col_acc[...] = part
            else:
                col_acc[...] += part
            weighted = following
        col_ref[:, at_j] = inverse_sq * (
            col_acc[0:FEATURES, :] - z_ref[:, at_j].astype(F32) * col_acc[FEATURES:FEATURES + 1, :]
        )

    @pl.loop(0, row_count // STRIP)
    def _(index_now):
        at = window(index_now, STRIP)
        row_ref[:, at] = inverse_sq * (
            row_acc[0:FEATURES, at] - x_ref[:, at].astype(F32) * row_acc[FEATURES + 3:FEATURES + 4, at]
        )


def shards(row_features, col_features, solve_rows, solve_cols, probe_rows, probe_cols):
    row_count, col_count = row_features.shape[1], col_features.shape[1]
    row_full = lax.all_gather(row_features, "col", axis=0, tiled=True)
    col_full = lax.all_gather(col_features, "row", axis=0, tiled=True)
    vmem = pl.BlockSpec(memory_space=pltpu.VMEM)
    row_part, col_part = pl.pallas_call(
        local_kernel,
        out_shape=(
            jax.ShapeDtypeStruct((FEATURES, row_count), F32),
            jax.ShapeDtypeStruct((FEATURES, col_count), F32),
        ),
        in_specs=[vmem] * 6,
        out_specs=(vmem, vmem),
        scratch_shapes=[
            pltpu.VMEM((WIDE, row_count), BF16),
            pltpu.VMEM((WIDE, col_count), BF16),
            pltpu.VMEM((row_count, WIDE), BF16),
            pltpu.VMEM((row_count, WEIGHT_ROWS), BF16),
            pltpu.VMEM((WEIGHT_ROWS, col_count), BF16),
            pltpu.VMEM((WIDE, row_count), F32),
            pltpu.VMEM((WIDE, COL_TILE), F32),
        ],
        compiler_params=pltpu.CompilerParams(vmem_limit_bytes=48 * 2**20),
        name="local_sweep",
    )(row_full, col_full, solve_rows[None, :], solve_cols[None, :], probe_rows, probe_cols)
    col_grad = lax.psum_scatter(col_part, "row", scatter_dimension=0, tiled=True)
    row_grad = lax.psum_scatter(row_part, "col", scatter_dimension=0, tiled=True)
    return (row_grad, col_grad)


def encode(values):
    peak = jnp.max(jnp.max(jnp.abs(values), 0, keepdims=True), 1, keepdims=True)
    scale = jnp.maximum(peak, 1e-35).astype(BF16).astype(F32)
    ratio = values * (1.0 / scale)
    square = ratio * ratio
    coded = square * square * square * ratio
    lanes = jnp.broadcast_to(scale, (values.shape[0], SCALE_LANES))
    return coded.astype(BF16), lanes.astype(BF16)


def decode(block):
    wide = block.astype(F32)
    coded, scale = wide[:, 0:COL_TILE], wide[:, COL_TILE:COL_TILE + 1]
    size = jnp.abs(coded)
    root = jnp.exp2(jnp.log(jnp.maximum(size, 1e-37)) * (LOG2E / 7.0)) * scale
    return jnp.where(size < 1e-37, 0.0, jnp.where(coded < 0.0, -root, root))


def fused_kernel(
    pair_count, x_ref, z_ref, sr_ref, sc_ref, pr_ref, pc_ref, row_ref, col_ref,
    x_aug, z_aug, x_turn, rw_turn, c_weight, row_acc, col_acc,
    col_part, pair_send, pair_recv, line_send, line_recv, row_send, row_recv,
    x_sems, own_send_sems, pass_send_sems, line_in, pair_in,
    pair_send_sem, pair_sum_in, line_send_sems, line_sum_in, row_send_sem, row_in,
    pr_held, pc_held, load_sems,
):
    inverse_sq = 4.0 / FEATURES
    row_count, col_count = x_ref.shape[1], z_ref.shape[1]
    x_rows, z_rows = x_ref.shape[0], z_ref.shape[0]
    row_tiles, chunks = row_count // ROW_TILE, col_count // COL_TILE
    others = pair_count - 1
    me_row, me_col = lax.axis_index("row"), lax.axis_index("col")
    side, place = lax.rem(me_row, 2), me_row // 2
    pair_row = 2 * place + 1 - side
    other_col = 1 - me_col

    def line_place(step):
        return lax.rem(place + step, pair_count)

    def piece(owner, size):
        return pl.ds(pl.multiple_of(owner * size, size), size)

    def send(src, dst, send_sem, recv_sem, where):
        return pltpu.make_async_remote_copy(
            src_ref=src, dst_ref=dst, send_sem=send_sem, recv_sem=recv_sem,
            device_id=where, device_id_type=pl.DeviceIdType.MESH,
        )

    barrier = pltpu.get_barrier_semaphore()
    partners = [{"col": other_col}, {"row": pair_row}]
    partners += [{"row": 2 * line_place(k) + side} for k in range(1, pair_count)]
    for partner in partners:
        pl.semaphore_signal(barrier, inc=1, device_id=partner, device_id_type=pl.DeviceIdType.MESH)
    pl.semaphore_wait(barrier, len(partners))

    my_x = piece(me_col, x_rows)
    x_copy = send(x_ref, x_aug.at[my_x, :], x_sems.at[0], x_sems.at[1], {"col": other_col})
    my_z = piece(me_row, z_rows)

    def own_copy(k, at, recv_sem):
        where = pair_row if k == 0 else 2 * line_place(k) + side
        return send(z_ref.at[:, at], z_aug.at[my_z, at], own_send_sems.at[k], recv_sem, {"row": where})

    def pass_copy(k, at, recv_sem):
        owner = piece(2 * line_place(k) + side, z_rows)
        return send(z_aug.at[owner, at], z_aug.at[owner, at], pass_send_sems.at[k - 1], recv_sem, {"row": pair_row})

    @pl.loop(0, chunks)
    def _(c):
        at = window(c, COL_TILE)
        for k in range(1, pair_count):
            own_copy(k, at, line_in.at[c]).start()
        own_copy(0, at, pair_in.at[c]).start()
        @pl.when(c == 0)
        def _():
            x_copy.start()

    def take_line(c):
        at = window(c, COL_TILE)
        got = z_aug.at[pl.ds(0, others * z_rows), at]
        pltpu.make_async_copy(got, got, line_in.at[c]).wait()
        for k in range(1, pair_count):
            pass_copy(k, at, pair_in.at[c]).start()

    def take_pair(c):
        got = z_aug.at[pl.ds(0, pair_count * z_rows), window(c, COL_TILE)]
        pltpu.make_async_copy(got, got, pair_in.at[c]).wait()

    loads = [
        pltpu.make_async_copy(src, dst, load_sems.at[n])
        for n, (src, dst) in enumerate(
            [(pr_ref, pr_held), (x_ref, x_aug.at[my_x, :]), (z_ref, z_aug.at[my_z, :]), (pc_ref, pc_held)]
        )
    ]
    for load in loads:
        load.start()
    loads[0].wait()

    @pl.loop(0, row_count // STRIP)
    def _(index_now):
        at = window(index_now, STRIP)
        rw_turn[at, :] = turned(weight_rows(sr_ref[:, at], pr_held[:, at], 0.5, -0.5 / PROBES, False))

    row_acc[...] = jnp.zeros_like(row_acc)
    for load in loads[1:]:
        load.wait()
    x_copy.wait_recv()

    @pl.loop(0, row_count // STRIP)
    def _(index_now):
        at = window(index_now, STRIP)
        x_aug[FEATURES:WIDE, at] = extra_rows(x_aug[0:FEATURES, at], False)
        x_turn[at, :] = turned(x_aug[:, at])

    for c in range(min(AHEAD, chunks)):
        take_line(c)

    def weighted_tile(i, at_j):
        at_i = pl.ds(i * ROW_TILE, ROW_TILE)
        half = jnp.dot(x_turn[at_i, :], z_aug[:, at_j], preferred_element_type=F32)
        coupling = jnp.dot(rw_turn[at_i, :], c_weight[...], preferred_element_type=F32)
        return (coupling * jnp.exp2(half * (inverse_sq * LOG2E))).astype(BF16)

    def pair_copy(c):
        return send(pair_send.at[c], pair_recv.at[c], pair_send_sem, pair_sum_in.at[c], {"row": pair_row})

    def line_copy(c, k):
        return send(
            line_send.at[c, k - 1], line_recv.at[c, k - 1], line_send_sems.at[k - 1], line_sum_in.at[c],
            {"row": 2 * line_place(k) + side},
        )

    def add_pair(c):
        pltpu.make_async_copy(pair_recv.at[c], pair_recv.at[c], pair_sum_in.at[c]).wait()
        for k in range(1, pair_count):
            there = line_place(k)
            total = col_part[c, piece(2 * there + side, z_rows), :] + decode(pair_recv[c, there])
            coded, scale = encode(total)
            line_send[c, k - 1, :, 0:COL_TILE] = coded
            line_send[c, k - 1, :, COL_TILE:COL_TILE + SCALE_LANES] = scale
            line_copy(c, k).start()

    def add_line(c):
        pltpu.make_async_copy(line_recv.at[c], line_recv.at[c], line_sum_in.at[c]).wait()
        total = col_part[c, my_z, :] + decode(pair_recv[c, place])
        for k in range(1, pair_count):
            total = total + decode(line_recv[c, k - 1])
        col_ref[:, window(c, COL_TILE)] = total

    @pl.loop(0, chunks)
    def _(c):
        at_j = window(c, COL_TILE)

        @pl.when(c + AHEAD < chunks)
        def _():
            take_line(c + AHEAD)

        c_weight[...] = weight_rows(sc_ref[:, at_j], pc_held[:, at_j], 1.0, 1.0, True)
        take_pair(c)
        z_aug[FEATURES:WIDE, at_j] = extra_rows(z_aug[0:FEATURES, at_j], True)
        weighted = weighted_tile(0, at_j)
        for i in range(row_tiles):
            following = weighted_tile(i + 1, at_j) if i + 1 < row_tiles else None
            at_i = pl.ds(i * ROW_TILE, ROW_TILE)
            row_acc[:, at_i] += lax.dot_general(
                z_aug[:, at_j], weighted, (((1,), (1,)), ((), ())), preferred_element_type=F32
            )
            part = jnp.dot(x_aug[:, at_i], weighted, preferred_element_type=F32)
            if i == 0:
                col_acc[...] = part
            else:
                col_acc[...] += part
            weighted = following
        col_part[c] = inverse_sq * (
            col_acc[0:FEATURES, :] - z_aug[0:FEATURES, at_j].astype(F32) * col_acc[FEATURES:FEATURES + 1, :]
        )
        for there in range(pair_count):
            coded, scale = encode(col_part[c, piece(2 * there + 1 - side, z_rows), :])
            pair_send[c, there, :, 0:COL_TILE] = coded
            pair_send[c, there, :, COL_TILE:COL_TILE + SCALE_LANES] = scale
        pair_copy(c).start()

        @pl.when(c >= 1)
        def _():
            add_pair(c - 1)

    def row_piece(owner, at):
        at_f = piece(owner, x_rows)
        return inverse_sq * (
            row_acc[at_f, at] - x_aug[at_f, at].astype(F32) * row_acc[FEATURES + 3:FEATURES + 4, at]
        )

    def row_copy(index_now):
        return send(
            row_send.at[index_now], row_recv.at[index_now], row_send_sem, row_in.at[index_now], {"col": other_col}
        )

    strips = row_count // STRIP

    @pl.loop(0, strips)
    def _(index_now):
        row_send[index_now] = row_piece(other_col, window(index_now, STRIP))
        row_copy(index_now).start()

    add_pair(chunks - 1)

    @pl.loop(0, chunks - 1)
    def _(c):
        add_line(c)

    @pl.loop(0, strips)
    def _(index_now):
        at = window(index_now, STRIP)
        row_copy(index_now).wait_recv()
        row_ref[:, at] = row_piece(me_col, at) + row_recv[index_now]

    add_line(chunks - 1)

    x_copy.wait_send()
    for k in range(pair_count):
        own_copy(k, pl.ds(0, col_count), line_in.at[0]).wait_send()
    for k in range(1, pair_count):
        pass_copy(k, pl.ds(0, col_count), pair_in.at[0]).wait_send()
        sent = line_send.at[:, k - 1]
        pltpu.make_async_copy(sent, sent, line_send_sems.at[k - 1]).wait()
    pltpu.make_async_copy(pair_send, pair_send, pair_send_sem).wait()
    pltpu.make_async_copy(row_send, row_send, row_send_sem).wait()


def fused_shards(rows, row_features, col_features, solve_rows, solve_cols, probe_rows, probe_cols):
    (x_rows, row_count), (z_rows, col_count) = row_features.shape, col_features.shape
    pair_count, chunks, strips = rows // 2, col_count // COL_TILE, row_count // STRIP
    vmem, hbm = pl.BlockSpec(memory_space=pltpu.VMEM), pl.BlockSpec(memory_space=pl.ANY)
    dma = pltpu.SemaphoreType.DMA
    return pl.pallas_call(
        functools.partial(fused_kernel, pair_count),
        out_shape=(
            jax.ShapeDtypeStruct((x_rows, row_count), F32),
            jax.ShapeDtypeStruct((z_rows, col_count), F32),
        ),
        in_specs=[hbm, hbm, vmem, vmem, hbm, hbm],
        out_specs=(vmem, vmem),
        scratch_shapes=[
            pltpu.VMEM((WIDE, row_count), BF16),
            pltpu.VMEM((WIDE, col_count), BF16),
            pltpu.VMEM((row_count, WIDE), BF16),
            pltpu.VMEM((row_count, WEIGHT_ROWS), BF16),
            pltpu.VMEM((WEIGHT_ROWS, COL_TILE), BF16),
            pltpu.VMEM((WIDE, row_count), F32),
            pltpu.VMEM((WIDE, COL_TILE), F32),
            pltpu.VMEM((chunks, FEATURES, COL_TILE), F32),
            pltpu.VMEM((chunks, pair_count, z_rows, COL_TILE + SCALE_LANES), BF16),
            pltpu.VMEM((chunks, pair_count, z_rows, COL_TILE + SCALE_LANES), BF16),
            pltpu.VMEM((chunks, pair_count - 1, z_rows, COL_TILE + SCALE_LANES), BF16),
            pltpu.VMEM((chunks, pair_count - 1, z_rows, COL_TILE + SCALE_LANES), BF16),
            pltpu.VMEM((strips, x_rows, STRIP), F32),
            pltpu.VMEM((strips, x_rows, STRIP), F32),
            dma((2,)),
            dma((pair_count,)),
            dma((pair_count - 1,)),
            dma((chunks,)),
            dma((chunks,)),
            dma,
            dma((chunks,)),
            dma((pair_count - 1,)),
            dma((chunks,)),
            dma,
            dma((strips,)),
            pltpu.VMEM((PROBES, row_count), F32),
            pltpu.VMEM((PROBES, col_count), F32),
            dma((4,)),
        ],
        compiler_params=pltpu.CompilerParams(
            collective_id=0, has_side_effects=True, vmem_limit_bytes=48 * 2**20
        ),
        name="fused_sweep",
    )(row_features, col_features, solve_rows[None, :], solve_cols[None, :], probe_rows, probe_cols)


def solution(mesh):
    rows = mesh.shape["row"]
    whole_tiles = (FEATURES // rows) % 16 == 0 and rows >= 4 and rows % 2 == 0 and mesh.shape["col"] == 2
    return jax.shard_map(
        functools.partial(fused_shards, rows) if whole_tiles else shards,
        mesh=mesh,
        in_specs=(
            P("col", ("pool", "row")),
            P("row", ("pool", "col")),
            P(("pool", "row")),
            P(("pool", "col")),
            P(None, ("pool", "row")),
            P(None, ("pool", "col")),
        ),
        out_specs=(P("col", ("pool", "row")), P("row", ("pool", "col"))),
        check_vma=False,
    )
```

```python
import functools

import jax
import jax.numpy as jnp
from jax import lax
from jax.experimental import pallas as pl
from jax.experimental.pallas import tpu as pltpu
from jax.sharding import PartitionSpec as P

FEATURES = 128
PROBES = 16
WIDE = FEATURES + 16
WEIGHT_ROWS = 64
STRIP = 512
ROW_TILE = 256
COL_TILE = 1024
AHEAD = 2
SCALE_LANES = 128
LOG2E = 1.4426950408889634
F32 = jnp.float32
BF16 = jnp.bfloat16


def split_parts(values, count):
    parts = []
    for _ in range(count - 1):
        high = values.astype(BF16).astype(F32)
        parts.append(high)
        values = values - high
    parts.append(values)
    return parts


def half_norm(features):
    wide = features.astype(F32)
    return jnp.concatenate(split_parts(-0.5 * jnp.sum(wide * wide, 0, keepdims=True), 3), 0)


def extra_rows(features, norm_first):
    count = features.shape[1]
    ones = jnp.ones((3, count), F32)
    pad = jnp.zeros((WIDE - FEATURES - 6, count), F32)
    norm = half_norm(features)
    rows = [norm, ones, pad] if norm_first else [ones, norm, pad]
    return jnp.concatenate(rows, 0).astype(BF16)


def weight_rows(solve, probe, solve_scale, probe_scale, low_last):
    high, low = split_parts(jnp.concatenate([solve_scale * solve, probe_scale * probe], 0), 2)
    pad = jnp.zeros((WEIGHT_ROWS - 3 * (PROBES + 1), solve.shape[1]), F32)
    parts = [high, high, low] if low_last else [high, low, high]
    return jnp.concatenate(parts + [pad], 0).astype(BF16)


def window(index_now, size):
    return pl.ds(pl.multiple_of(index_now * size, size), size)


def turned(values):
    return values.astype(F32).T.astype(BF16)


def local_kernel(
    x_ref, z_ref, sr_ref, sc_ref, pr_ref, pc_ref, row_ref, col_ref,
    x_aug, z_aug, x_turn, rw_turn, c_weight, row_acc, col_acc,
):
    inverse_sq = 4.0 / FEATURES
    row_count, col_count = x_ref.shape[1], z_ref.shape[1]
    row_tiles = row_count // ROW_TILE

    @pl.loop(0, row_count // STRIP)
    def _(index_now):
        at = window(index_now, STRIP)
        x = x_ref[:, at]
        x_aug[0:FEATURES, at] = x
        x_aug[FEATURES:WIDE, at] = extra_rows(x, False)
        x_turn[at, :] = turned(x_aug[:, at])
        rw_turn[at, :] = turned(weight_rows(sr_ref[:, at], pr_ref[:, at], 0.5, -0.5 / PROBES, False))

    @pl.loop(0, col_count // STRIP)
    def _(index_now):
        at = window(index_now, STRIP)
        z = z_ref[:, at]
        z_aug[0:FEATURES, at] = z
        z_aug[FEATURES:WIDE, at] = extra_rows(z, True)
        c_weight[:, at] = weight_rows(sc_ref[:, at], pc_ref[:, at], 1.0, 1.0, True)

    row_acc[...] = jnp.zeros_like(row_acc)

    def weighted_tile(i, at_j):
        at_i = pl.ds(i * ROW_TILE, ROW_TILE)
        half = jnp.dot(x_turn[at_i, :], z_aug[:, at_j], preferred_element_type=F32)
        coupling = jnp.dot(rw_turn[at_i, :], c_weight[:, at_j], preferred_element_type=F32)
        return (coupling * jnp.exp2(half * (inverse_sq * LOG2E))).astype(BF16)

    @pl.loop(0, col_count // COL_TILE)
    def _(j):
        at_j = window(j, COL_TILE)
        weighted = weighted_tile(0, at_j)
        for i in range(row_tiles):
            following = weighted_tile(i + 1, at_j) if i + 1 < row_tiles else None
            at_i = pl.ds(i * ROW_TILE, ROW_TILE)
            row_acc[:, at_i] += lax.dot_general(
                z_aug[:, at_j], weighted, (((1,), (1,)), ((), ())), preferred_element_type=F32
            )
            part = jnp.dot(x_aug[:, at_i], weighted, preferred_element_type=F32)
            if i == 0:
                col_acc[...] = part
            else:
                col_acc[...] += part
            weighted = following
        col_ref[:, at_j] = inverse_sq * (
            col_acc[0:FEATURES, :] - z_ref[:, at_j].astype(F32) * col_acc[FEATURES:FEATURES + 1, :]
        )

    @pl.loop(0, row_count // STRIP)
    def _(index_now):
        at = window(index_now, STRIP)
        row_ref[:, at] = inverse_sq * (
            row_acc[0:FEATURES, at] - x_ref[:, at].astype(F32) * row_acc[FEATURES + 3:FEATURES + 4, at]
        )


def shards(row_features, col_features, solve_rows, solve_cols, probe_rows, probe_cols):
    row_count, col_count = row_features.shape[1], col_features.shape[1]
    row_full = lax.all_gather(row_features, "col", axis=0, tiled=True)
    col_full = lax.all_gather(col_features, "row", axis=0, tiled=True)
    vmem = pl.BlockSpec(memory_space=pltpu.VMEM)
    row_part, col_part = pl.pallas_call(
        local_kernel,
        out_shape=(
            jax.ShapeDtypeStruct((FEATURES, row_count), F32),
            jax.ShapeDtypeStruct((FEATURES, col_count), F32),
        ),
        in_specs=[vmem] * 6,
        out_specs=(vmem, vmem),
        scratch_shapes=[
            pltpu.VMEM((WIDE, row_count), BF16),
            pltpu.VMEM((WIDE, col_count), BF16),
            pltpu.VMEM((row_count, WIDE), BF16),
            pltpu.VMEM((row_count, WEIGHT_ROWS), BF16),
            pltpu.VMEM((WEIGHT_ROWS, col_count), BF16),
            pltpu.VMEM((WIDE, row_count), F32),
            pltpu.VMEM((WIDE, COL_TILE), F32),
        ],
        compiler_params=pltpu.CompilerParams(vmem_limit_bytes=48 * 2**20),
        name="local_sweep",
    )(row_full, col_full, solve_rows[None, :], solve_cols[None, :], probe_rows, probe_cols)
    col_grad = lax.psum_scatter(col_part, "row", scatter_dimension=0, tiled=True)
    row_grad = lax.psum_scatter(row_part, "col", scatter_dimension=0, tiled=True)
    return (row_grad, col_grad)


def encode(values):
    peak = jnp.max(jnp.max(jnp.abs(values), 0, keepdims=True), 1, keepdims=True)
    scale = jnp.maximum(peak, 1e-35).astype(BF16).astype(F32)
    ratio = values * (1.0 / scale)
    square = ratio * ratio
    coded = square * square * square * ratio
    lanes = jnp.broadcast_to(scale, (values.shape[0], SCALE_LANES))
    return coded.astype(BF16), lanes.astype(BF16)


def decode(block):
    wide = block.astype(F32)
    coded, scale = wide[:, 0:COL_TILE], wide[:, COL_TILE:COL_TILE + 1]
    size = jnp.abs(coded)
    root = jnp.exp2(jnp.log(jnp.maximum(size, 1e-37)) * (LOG2E / 7.0)) * scale
    return jnp.where(size < 1e-37, 0.0, jnp.where(coded < 0.0, -root, root))


def fused_kernel(
    pair_count, x_ref, z_ref, sr_ref, sc_ref, pr_ref, pc_ref, row_ref, col_ref,
    x_aug, z_aug, x_turn, rw_turn, c_weight, row_acc, col_acc,
    col_part, pair_send, pair_recv, line_send, line_recv, row_send, row_recv,
    x_sems, own_send_sems, pass_send_sems, line_in, pair_in,
    pair_send_sem, pair_sum_in, line_send_sems, line_sum_in, row_send_sem, row_in,
    pr_held, pc_held, load_sems,
):
    inverse_sq = 4.0 / FEATURES
    row_count, col_count = x_ref.shape[1], z_ref.shape[1]
    x_rows, z_rows = x_ref.shape[0], z_ref.shape[0]
    row_tiles, chunks = row_count // ROW_TILE, col_count // COL_TILE
    others = pair_count - 1
    me_row, me_col = lax.axis_index("row"), lax.axis_index("col")
    side, place = lax.rem(me_row, 2), me_row // 2
    pair_row = 2 * place + 1 - side
    other_col = 1 - me_col

    def line_place(step):
        return lax.rem(place + step, pair_count)

    def piece(owner, size):
        return pl.ds(pl.multiple_of(owner * size, size), size)

    def send(src, dst, send_sem, recv_sem, where):
        return pltpu.make_async_remote_copy(
            src_ref=src, dst_ref=dst, send_sem=send_sem, recv_sem=recv_sem,
            device_id=where, device_id_type=pl.DeviceIdType.MESH,
        )

    barrier = pltpu.get_barrier_semaphore()
    partners = [{"col": other_col}, {"row": pair_row}]
    partners += [{"row": 2 * line_place(k) + side} for k in range(1, pair_count)]
    for partner in partners:
        pl.semaphore_signal(barrier, inc=1, device_id=partner, device_id_type=pl.DeviceIdType.MESH)
    pl.semaphore_wait(barrier, len(partners))

    my_x = piece(me_col, x_rows)
    x_copy = send(x_ref, x_aug.at[my_x, :], x_sems.at[0], x_sems.at[1], {"col": other_col})
    my_z = piece(me_row, z_rows)

    def own_copy(k, at, recv_sem):
        where = pair_row if k == 0 else 2 * line_place(k) + side
        return send(z_ref.at[:, at], z_aug.at[my_z, at], own_send_sems.at[k], recv_sem, {"row": where})

    def pass_copy(k, at, recv_sem):
        owner = piece(2 * line_place(k) + side, z_rows)
        return send(z_aug.at[owner, at], z_aug.at[owner, at], pass_send_sems.at[k - 1], recv_sem, {"row": pair_row})

    @pl.loop(0, chunks)
    def _(c):
        at = window(c, COL_TILE)
        for k in range(1, pair_count):
            own_copy(k, at, line_in.at[c]).start()
        own_copy(0, at, pair_in.at[c]).start()
        @pl.when(c == 0)
        def _():
            x_copy.start()

    def take_line(c):
        at = window(c, COL_TILE)
        got = z_aug.at[pl.ds(0, others * z_rows), at]
        pltpu.make_async_copy(got, got, line_in.at[c]).wait()
        for k in range(1, pair_count):
            pass_copy(k, at, pair_in.at[c]).start()

    def take_pair(c):
        got = z_aug.at[pl.ds(0, pair_count * z_rows), window(c, COL_TILE)]
        pltpu.make_async_copy(got, got, pair_in.at[c]).wait()

    loads = [
        pltpu.make_async_copy(src, dst, load_sems.at[n])
        for n, (src, dst) in enumerate(
            [(pr_ref, pr_held), (x_ref, x_aug.at[my_x, :]), (z_ref, z_aug.at[my_z, :]), (pc_ref, pc_held)]
        )
    ]
    for load in loads:
        load.start()
    loads[0].wait()

    @pl.loop(0, row_count // STRIP)
    def _(index_now):
        at = window(index_now, STRIP)
        rw_turn[at, :] = turned(weight_rows(sr_ref[:, at], pr_held[:, at], 0.5, -0.5 / PROBES, False))

    take_line(0)
    row_acc[...] = jnp.zeros_like(row_acc)
    for load in loads[1:]:
        load.wait()
    x_copy.wait_recv()

    @pl.loop(0, row_count // STRIP)
    def _(index_now):
        at = window(index_now, STRIP)
        x_aug[FEATURES:WIDE, at] = extra_rows(x_aug[0:FEATURES, at], False)
        x_turn[at, :] = turned(x_aug[:, at])

    for c in range(1, min(AHEAD, chunks)):
        take_line(c)

    def weighted_tile(i, at_j):
        at_i = pl.ds(i * ROW_TILE, ROW_TILE)
        half = jnp.dot(x_turn[at_i, :], z_aug[:, at_j], preferred_element_type=F32)
        coupling = jnp.dot(rw_turn[at_i, :], c_weight[...], preferred_element_type=F32)
        return (coupling * jnp.exp2(half * (inverse_sq * LOG2E))).astype(BF16)

    def pair_copy(c):
        return send(pair_send.at[c], pair_recv.at[c], pair_send_sem, pair_sum_in.at[c], {"row": pair_row})

    def line_copy(c, k):
        return send(
            line_send.at[c, k - 1], line_recv.at[c, k - 1], line_send_sems.at[k - 1], line_sum_in.at[c],
            {"row": 2 * line_place(k) + side},
        )

    def add_pair(c):
        pltpu.make_async_copy(pair_recv.at[c], pair_recv.at[c], pair_sum_in.at[c]).wait()
        for k in range(1, pair_count):
            there = line_place(k)
            total = col_part[c, piece(2 * there + side, z_rows), :] + decode(pair_recv[c, there])
            coded, scale = encode(total)
            line_send[c, k - 1, :, 0:COL_TILE] = coded
            line_send[c, k - 1, :, COL_TILE:COL_TILE + SCALE_LANES] = scale
            line_copy(c, k).start()

    def add_line(c):
        pltpu.make_async_copy(line_recv.at[c], line_recv.at[c], line_sum_in.at[c]).wait()
        total = col_part[c, my_z, :] + decode(pair_recv[c, place])
        for k in range(1, pair_count):
            total = total + decode(line_recv[c, k - 1])
        col_ref[:, window(c, COL_TILE)] = total

    @pl.loop(0, chunks)
    def _(c):
        at_j = window(c, COL_TILE)

        @pl.when(c + AHEAD < chunks)
        def _():
            take_line(c + AHEAD)

        c_weight[...] = weight_rows(sc_ref[:, at_j], pc_held[:, at_j], 1.0, 1.0, True)
        take_pair(c)
        z_aug[FEATURES:WIDE, at_j] = extra_rows(z_aug[0:FEATURES, at_j], True)
        weighted = weighted_tile(0, at_j)
        for i in range(row_tiles):
            following = weighted_tile(i + 1, at_j) if i + 1 < row_tiles else None
            at_i = pl.ds(i * ROW_TILE, ROW_TILE)
            row_acc[:, at_i] += lax.dot_general(
                z_aug[:, at_j], weighted, (((1,), (1,)), ((), ())), preferred_element_type=F32
            )
            part = jnp.dot(x_aug[:, at_i], weighted, preferred_element_type=F32)
            if i == 0:
                col_acc[...] = part
            else:
                col_acc[...] += part
            weighted = following
        col_part[c] = inverse_sq * (
            col_acc[0:FEATURES, :] - z_aug[0:FEATURES, at_j].astype(F32) * col_acc[FEATURES:FEATURES + 1, :]
        )
        for there in range(pair_count):
            coded, scale = encode(col_part[c, piece(2 * there + 1 - side, z_rows), :])
            pair_send[c, there, :, 0:COL_TILE] = coded
            pair_send[c, there, :, COL_TILE:COL_TILE + SCALE_LANES] = scale
        pair_copy(c).start()

        @pl.when(c >= 1)
        def _():
            add_pair(c - 1)

    def row_piece(owner, at):
        at_f = piece(owner, x_rows)
        return inverse_sq * (
            row_acc[at_f, at] - x_aug[at_f, at].astype(F32) * row_acc[FEATURES + 3:FEATURES + 4, at]
        )

    def row_copy(index_now):
        return send(
            row_send.at[index_now], row_recv.at[index_now], row_send_sem, row_in.at[index_now], {"col": other_col}
        )

    strips = row_count // STRIP

    @pl.loop(0, strips)
    def _(index_now):
        row_send[index_now] = row_piece(other_col, window(index_now, STRIP))
        row_copy(index_now).start()

    add_pair(chunks - 1)

    @pl.loop(0, chunks - 1)
    def _(c):
        add_line(c)

    @pl.loop(0, strips)
    def _(index_now):
        at = window(index_now, STRIP)
        row_copy(index_now).wait_recv()
        row_ref[:, at] = row_piece(me_col, at) + row_recv[index_now]

    add_line(chunks - 1)

    x_copy.wait_send()
    for k in range(pair_count):
        own_copy(k, pl.ds(0, col_count), line_in.at[0]).wait_send()
    for k in range(1, pair_count):
        pass_copy(k, pl.ds(0, col_count), pair_in.at[0]).wait_send()
        sent = line_send.at[:, k - 1]
        pltpu.make_async_copy(sent, sent, line_send_sems.at[k - 1]).wait()
    pltpu.make_async_copy(pair_send, pair_send, pair_send_sem).wait()
    pltpu.make_async_copy(row_send, row_send, row_send_sem).wait()


def fused_shards(rows, row_features, col_features, solve_rows, solve_cols, probe_rows, probe_cols):
    (x_rows, row_count), (z_rows, col_count) = row_features.shape, col_features.shape
    pair_count, chunks, strips = rows // 2, col_count // COL_TILE, row_count // STRIP
    vmem, hbm = pl.BlockSpec(memory_space=pltpu.VMEM), pl.BlockSpec(memory_space=pl.ANY)
    dma = pltpu.SemaphoreType.DMA
    return pl.pallas_call(
        functools.partial(fused_kernel, pair_count),
        out_shape=(
            jax.ShapeDtypeStruct((x_rows, row_count), F32),
            jax.ShapeDtypeStruct((z_rows, col_count), F32),
        ),
        in_specs=[hbm, hbm, vmem, vmem, hbm, hbm],
        out_specs=(vmem, vmem),
        scratch_shapes=[
            pltpu.VMEM((WIDE, row_count), BF16),
            pltpu.VMEM((WIDE, col_count), BF16),
            pltpu.VMEM((row_count, WIDE), BF16),
            pltpu.VMEM((row_count, WEIGHT_ROWS), BF16),
            pltpu.VMEM((WEIGHT_ROWS, COL_TILE), BF16),
            pltpu.VMEM((WIDE, row_count), F32),
            pltpu.VMEM((WIDE, COL_TILE), F32),
            pltpu.VMEM((chunks, FEATURES, COL_TILE), F32),
            pltpu.VMEM((chunks, pair_count, z_rows, COL_TILE + SCALE_LANES), BF16),
            pltpu.VMEM((chunks, pair_count, z_rows, COL_TILE + SCALE_LANES), BF16),
            pltpu.VMEM((chunks, pair_count - 1, z_rows, COL_TILE + SCALE_LANES), BF16),
            pltpu.VMEM((chunks, pair_count - 1, z_rows, COL_TILE + SCALE_LANES), BF16),
            pltpu.VMEM((strips, x_rows, STRIP), F32),
            pltpu.VMEM((strips, x_rows, STRIP), F32),
            dma((2,)),
            dma((pair_count,)),
            dma((pair_count - 1,)),
            dma((chunks,)),
            dma((chunks,)),
            dma,
            dma((chunks,)),
            dma((pair_count - 1,)),
            dma((chunks,)),
            dma,
            dma((strips,)),
            pltpu.VMEM((PROBES, row_count), F32),
            pltpu.VMEM((PROBES, col_count), F32),
            dma((4,)),
        ],
        compiler_params=pltpu.CompilerParams(
            collective_id=0, has_side_effects=True, vmem_limit_bytes=48 * 2**20
        ),
        name="fused_sweep",
    )(row_features, col_features, solve_rows[None, :], solve_cols[None, :], probe_rows, probe_cols)


def solution(mesh):
    rows = mesh.shape["row"]
    whole_tiles = (FEATURES // rows) % 16 == 0 and rows >= 4 and rows % 2 == 0 and mesh.shape["col"] == 2
    return jax.shard_map(
        functools.partial(fused_shards, rows) if whole_tiles else shards,
        mesh=mesh,
        in_specs=(
            P("col", ("pool", "row")),
            P("row", ("pool", "col")),
            P(("pool", "row")),
            P(("pool", "col")),
            P(None, ("pool", "row")),
            P(None, ("pool", "col")),
        ),
        out_specs=(P("col", ("pool", "row")), P("row", ("pool", "col"))),
        check_vma=False,
    )
```
